32 devices in a mesh: dp: 8 (over z, y), mp: 4 (over x, core).
Axes of the slice: x: 2, y: 2, z: 4, core: 2. Of those that a mesh axis runs over, the one named last changes fastest.
Arguments:
- token_ids: int32 [128, 64], P(('dp', 'mp')), may hold values from 0 to 501152, as said below
- pair_index: int32 [64, 2], replicated, may hold values from 0 to 127, as said below
- table: bfloat16 [501248, 768], P(('dp', 'mp')), may hold values from -6 to 6
- query_key_value_weight: bfloat16 [768, 3, 768], P(None, None, 'mp'), may hold values from -0.21875 to 0.21875
- b_q: bfloat16 [768], P('mp'), may hold values from -3 to 3
- b_v: bfloat16 [768], P('mp'), may hold values from -3 to 3
- attention_output_weight: bfloat16 [768, 768], P('mp'), may hold values from -0.875 to 0.875
- b_o: bfloat16 [768], replicated, may hold values from -3 to 3
- ln1_gain: bfloat16 [768], replicated, may hold values from 0.25 to 1.75
- ln1_bias: bfloat16 [768], replicated, may hold values from -3 to 3
- feed_input_weight: bfloat16 [768, 3072], P(None, 'mp'), may hold values from -0.21875 to 0.21875
- feed_input_bias: bfloat16 [3072], P('mp'), may hold values from -3 to 3
- feed_output_weight: bfloat16 [3072, 768], P('mp'), may hold values from -0.15625 to 0.15625
- b_out: bfloat16 [768], replicated, may hold values from -3 to 3
- ln2_gain: bfloat16 [768], replicated, may hold values from 0.25 to 1.75
- ln2_bias: bfloat16 [768], replicated, may hold values from -3 to 3
- grad_out: float32 [128, 64, 768], P(('dp', 'mp')), may hold values from -6 to 6
Outputs:
- hidden: float32 [128, 64, 768], P(('dp', 'mp'))
- ranking_loss: float32 [], replicated
- table_grad: float32 [501248, 768], P(('dp', 'mp'))
- qkv_grad: float32 [768, 3, 768], P('dp', None, 'mp')
- q_bias_grad: float32 [768], P(('dp', 'mp'))
- v_bias_grad: float32 [768], P(('dp', 'mp'))
- o_grad: float32 [768, 768], P('mp', 'dp')
- o_bias_grad: float32 [768], P(('dp', 'mp'))
- ln1_gain_grad: float32 [768], P(('dp', 'mp'))
- ln1_bias_grad: float32 [768], P(('dp', 'mp'))
- in_grad: float32 [768, 3072], P('dp', 'mp')
- in_bias_grad: float32 [3072], P(('dp', 'mp'))
- out_grad: float32 [3072, 768], P('mp', 'dp')
- out_bias_grad: float32 [768], P(('dp', 'mp'))
- ln2_gain_grad: float32 [768], P(('dp', 'mp'))
- ln2_bias_grad: float32 [768], P(('dp', 'mp'))
The draws below stay inside these ranges and needn't reach their ends.
Inputs may be any that keep to these rules, and one draw needn't show every extreme that they name: `token_ids`: ids name rows among the first 501153 of the 501248 table rows. Among the tokens of one device (an aligned block of 4 sentences), at most 16 ids lie in any one range of 15664 rows; one range holds exactly 16 ids of every device's block. `pair_index`: each of the 128 sentences appears exactly once.
All inputs are finite; a program needn't handle non-finite values.
Results may differ from the reference program's by a relative error of at most 0.018.
The reference program's roundings to bfloat16 on the way count: a program that leaves them out, or rounds other values in their place, can miss the bound.
Values may be sent and summed in bfloat16 or wider, within the bound.
No kernel may reach another device: no remote copies, remote signals or barrier semaphores. Data moves between devices by JAX's collectives and lax.ppermute only.
A program may use at most 192 MiB of HBM per device.

```python
import jax
import jax.numpy as jnp
from jax import lax

D = 768
HEADS = 12
HEAD_DIM = 64
FF = 3072
LIVE = 501153
VOCAB = 501248
LEN = 64
SENT_SP = 4
GROUP = 16
SENTENCES = 128
PAIRS = 64
N_DP = 8
N_MP = 4


def draw_token_ids(key, part):
    shards = N_DP * N_MP
    block_len = SENT_SP * LEN
    capacity = 2 * block_len // shards
    rows_shard = VOCAB // shards
    assignment_count = shards * capacity
    owner_key, global_key, blocks_key = jax.random.split(key, 3)
    frequent_entry_holder = jax.random.randint(owner_key, (shards,), 0, 4) == 0
    shared_portion = jax.random.randint(global_key, (), 0, shards)
    assigned_device_index = jnp.arange(assignment_count, dtype=jnp.int32) // capacity
    last_rows = rows_shard - (VOCAB - LIVE)

    def one_block(block_key):
        pick_key, ranking_seed, order_key, row_key = jax.random.split(block_key, 4)
        selected_positions = jax.random.randint(pick_key, (), 0, shards)
        extra_credit = jnp.where(frequent_entry_holder[assigned_device_index], 32768, 0) + jnp.where((assigned_device_index == selected_positions) | (assigned_device_index == shared_portion), 65536, 0)
        ordering_measure = (jax.random.randint(ranking_seed, (assignment_count,), 0, 32768) + extra_credit) * 4096 + jnp.arange(assignment_count, dtype=jnp.int32)
        taken = lax.top_k(ordering_measure, block_len)[1].astype(jnp.int32)
        taken = taken[jax.random.permutation(order_key, block_len)]
        owners = taken // capacity
        limit = jnp.where(owners == shards - 1, last_rows, rows_shard)
        hot_limit = jnp.maximum(jnp.minimum(limit, rows_shard // 8), 1)
        bound = jnp.where(frequent_entry_holder[owners], hot_limit, limit)
        row_pick = jax.random.randint(row_key, (block_len,), 0, bound)
        return (owners * rows_shard + row_pick).reshape(SENT_SP, LEN)
    block_keys = jax.random.split(blocks_key, shards)
    return jax.vmap(one_block)(block_keys).reshape(SENTENCES, LEN).astype(jnp.int32)


def draw_pair_index(key, part):
    order = jax.random.permutation(jax.random.fold_in(key, 7), SENTENCES)
    return order.reshape(PAIRS, 2).astype(jnp.int32)


def steps_of(key, dims, cuts, smallest, largest):
    gain, own = 1.0, jax.random.fold_in(key, 6)
    for axis_at, parts in cuts:
        heights = jnp.exp(jax.random.uniform(jax.random.fold_in(own, axis_at), (parts,), jnp.float32, smallest / len(cuts), largest / len(cuts)))
        gain = gain * jnp.repeat(heights, dims[axis_at] // parts).reshape([-1 if axis == axis_at else 1 for axis in range(len(dims))])
    return gain


def gaussian(own_key, dims, scale, most, cuts=(), kind=jnp.bfloat16):
    drawn = scale * jax.random.normal(own_key, dims, jnp.float32)
    if cuts:
        drawn = drawn * steps_of(own_key, dims, cuts, -0.22, 0.18)
    return jnp.clip(drawn, -most, most).astype(kind)


def setup_inputs(seed: int = 0) -> dict:
    streams_of = jax.random.split(jax.random.key(seed), 18)
    token_ids = draw_token_ids(jax.random.fold_in(streams_of[17], 71), 0)
    pair_index = draw_pair_index(jax.random.fold_in(streams_of[17], 71), 0)
    table = gaussian(streams_of[2], (VOCAB, D), 1.0, 6.0, ((0, 32),))
    query_key_value_weight = gaussian(streams_of[3], (D, 3, D), D ** -0.5, 0.21875, ((2, 4),))
    b_q = gaussian(streams_of[4], (D,), 0.5, 3.0, ((0, 4),))
    b_v = gaussian(streams_of[5], (D,), 0.5, 3.0, ((0, 4),))
    attention_output_weight = gaussian(streams_of[6], (D, D), (D // 16) ** -0.5, 0.875, ((0, 4),))
    b_o = gaussian(streams_of[7], (D,), 0.5, 3.0)
    ln1_gain = jnp.clip(1.0 + 0.15 * jax.random.normal(streams_of[8], (D,), jnp.float32), 0.25, 1.75).astype(jnp.bfloat16)
    ln1_bias = gaussian(streams_of[9], (D,), 0.5, 3.0)
    feed_input_weight = gaussian(streams_of[10], (D, FF), D ** -0.5, 0.21875, ((1, 4),))
    feed_input_bias = gaussian(streams_of[11], (FF,), 0.5, 3.0, ((0, 4),))
    feed_output_weight = gaussian(streams_of[12], (FF, D), (FF // 2) ** -0.5, 0.15625, ((0, 4),))
    b_out = gaussian(streams_of[13], (D,), 0.5, 3.0)
    ln2_gain = jnp.clip(1.0 + 0.15 * jax.random.normal(streams_of[14], (D,), jnp.float32), 0.25, 1.75).astype(jnp.bfloat16)
    ln2_bias = gaussian(streams_of[15], (D,), 0.5, 3.0)
    grad_out = gaussian(streams_of[16], (SENTENCES, LEN, D), 1.0, 6.0, ((0, 32),), jnp.float32)
    return dict(token_ids=token_ids, pair_index=pair_index, table=table, query_key_value_weight=query_key_value_weight, b_q=b_q, b_v=b_v, attention_output_weight=attention_output_weight, b_o=b_o, ln1_gain=ln1_gain, ln1_bias=ln1_bias, feed_input_weight=feed_input_weight, feed_input_bias=feed_input_bias, feed_output_weight=feed_output_weight, b_out=b_out, ln2_gain=ln2_gain, ln2_bias=ln2_bias, grad_out=grad_out)


@jax.custom_vjp
def lower_precision(v):
    return lax.optimization_barrier(v.astype(jnp.bfloat16)).astype(jnp.float32)

@jax.custom_vjp
def lower_precision_back(v):
    return v

def low_keep(v):
    return (lower_precision(v), None)

def low_pass(kept, grad):
    return (grad,)

def back_keep(v):
    return (v, None)

def back_low(kept, grad):
    return (lower_precision(grad),)
lower_precision.defvjp(low_keep, low_pass)
lower_precision_back.defvjp(back_keep, back_low)
highest_value = lax.Precision.HIGHEST
norm_eps = 1e-06
score_scale = 50.0
margin = 0.3

def norm_rows(array_in, gain_vec, shift_vec):
    centre = array_in - lax.optimization_barrier(jnp.mean(array_in, axis=-1, keepdims=True))
    inverse = lax.rsqrt(lax.optimization_barrier(jnp.mean(centre * centre, axis=-1, keepdims=True)) + norm_eps)
    return centre * inverse * gain_vec + shift_vec

def layer_group(embedded_tokens, query_key_value_weight, b_q, b_v, attention_output_weight, b_o, gain_one, shift_one, feed_input_weight, feed_input_bias, feed_output_weight, b_out, gain_two, shift_two):
    sent_count = embedded_tokens.shape[0]
    mixed_output = jnp.einsum('nat,tjh->najh', embedded_tokens, query_key_value_weight, precision=highest_value)
    queries = lower_precision_back(lower_precision(mixed_output[:, :, 0] + b_q)).reshape(sent_count, LEN, HEADS, HEAD_DIM)
    key_rows = lower_precision_back(lower_precision(mixed_output[:, :, 1])).reshape(sent_count, LEN, HEADS, HEAD_DIM)
    values = lower_precision_back(lower_precision(mixed_output[:, :, 2] + b_v)).reshape(sent_count, LEN, HEADS, HEAD_DIM)
    scores = lower_precision_back(jnp.einsum('slhd,smhd->shlm', queries, key_rows, precision=highest_value) * HEAD_DIM ** (-0.5))
    row_peak = lax.optimization_barrier(jnp.max(scores, axis=-1, keepdims=True))
    weights = jnp.exp(scores - row_peak)
    prob_low = lower_precision(weights / lax.optimization_barrier(jnp.sum(weights, axis=-1, keepdims=True)))
    context_rows = jnp.einsum('shlm,smhd->slhd', prob_low, values, precision=highest_value).reshape(sent_count, LEN, D)
    context_rows = lower_precision_back(lower_precision(context_rows))
    attention_mixed_rows = lower_precision_back(jnp.einsum('hug,gi->hui', context_rows, attention_output_weight, precision=highest_value))
    first_normed_rows = norm_rows(embedded_tokens + attention_mixed_rows + b_o, gain_one, shift_one)
    up_projected = lower_precision_back(jnp.einsum('hku,un->hkn', lower_precision(first_normed_rows), feed_input_weight, precision=highest_value) + feed_input_bias)
    gelu_activations = lower_precision(jax.nn.gelu(up_projected, approximate=False))
    feed_forward_branch = lower_precision_back(jnp.einsum('tzb,bi->tzi', gelu_activations, feed_output_weight, precision=highest_value))
    return norm_rows(first_normed_rows + feed_forward_branch + b_out, gain_two, shift_two)

def reference(token_ids, pair_index, table, query_key_value_weight, b_q, b_v, attention_output_weight, b_o, ln1_gain, ln1_bias, feed_input_weight, feed_input_bias, feed_output_weight, b_out, ln2_gain, ln2_bias, grad_out):
    inputs = tuple((item.astype(jnp.float32) for item in (table, query_key_value_weight, b_q, b_v, attention_output_weight, b_o, ln1_gain, ln1_bias, feed_input_weight, feed_input_bias, feed_output_weight, b_out, ln2_gain, ln2_bias)))

    def objective(table_full, *weight_list):
        embedded_tokens = jnp.take(table_full, token_ids.reshape(-1), axis=0).reshape(N_DP, GROUP, LEN, D)

        def group_step(group_rows):
            return layer_group(group_rows, *weight_list)
        hidden = lax.map(jax.checkpoint(group_step), embedded_tokens).reshape(SENTENCES, LEN, D)
        cls_rows = hidden[:, 0, :]
        pooled = lower_precision(cls_rows * lax.rsqrt(lax.optimization_barrier(jnp.sum(cls_rows * cls_rows, axis=-1, keepdims=True)) + norm_eps))
        source = pooled[pair_index[:, 0]]
        target = pooled[pair_index[:, 1]]
        eye_pairs = jnp.eye(PAIRS, dtype=jnp.float32)
        logits = score_scale * (jnp.dot(source, target.T, precision=highest_value) - margin * eye_pairs)
        row_peak = lax.optimization_barrier(jnp.max(logits, axis=1, keepdims=True))
        row_lse = row_peak[:, 0] + jnp.log(lax.optimization_barrier(jnp.sum(jnp.exp(logits - row_peak), axis=1)))
        col_peak = lax.optimization_barrier(jnp.max(logits, axis=0, keepdims=True))
        col_lse = col_peak[0] + jnp.log(lax.optimization_barrier(jnp.sum(jnp.exp(logits - col_peak), axis=0)))
        loss_sum = 0.5 * jnp.sum(row_lse + col_lse) - jnp.sum(jnp.diagonal(logits))
        return (hidden, loss_sum)
    (hidden, loss_sum), pull = jax.vjp(objective, *inputs)
    grads = pull((grad_out.astype(jnp.float32), jnp.ones((), jnp.float32)))
    return (hidden, loss_sum / PAIRS, grads[0], grads[1], grads[2], grads[3], grads[4], grads[5], grads[6], grads[7], grads[8], grads[9], grads[10], grads[11], grads[12], grads[13])
```

```python
import functools

import jax
import jax.numpy as jnp
from jax import lax
from jax.experimental import pallas as pl
from jax.experimental.pallas import tpu as pltpu
from jax.sharding import PartitionSpec as P

HEAD_DIM = 64

norm_eps = 1e-06
score_scale = 50.0
margin = 0.3
root_half = 0.7071067811865476
inv_root_tau = 0.3989422804014327
highest_value = lax.Precision.HIGHEST
masked_out = -1e30

bf16 = jnp.bfloat16
f32 = jnp.float32
VMEM_LIMIT = 60 * 1024 * 1024


def dot(a, b):
    return jnp.dot(a, b, preferred_element_type=f32)


def dot_nt(a, b):
    return lax.dot_general(a, b, (((1,), (1,)), ((), ())), preferred_element_type=f32)


def dot_tn(a, b):
    return lax.dot_general(a, b, (((0,), (0,)), ((), ())), preferred_element_type=f32)


def mean_rows(v):
    return jnp.mean(v, axis=-1, keepdims=True)


def head_mask(rows, cols, head):
    lane = lax.broadcasted_iota(jnp.int32, (rows, cols), 1)
    return ((lane >= head * HEAD_DIM) & (lane < (head + 1) * HEAD_DIM)).astype(bf16)


def front_kernel(
    seq, fetched, pos, a0, a1, a2, a3, vec, x_out, qkv_out, prob_out, ctx_out, norm_out, inv_out,
    bias_out,
):
    tok, width = x_out.shape
    slots = fetched.shape[0]
    hc = ctx_out.shape[2]
    heads = hc // HEAD_DIM
    span = 2 * seq
    spans = tok // span
    hot = (lax.broadcasted_iota(jnp.int32, (tok, slots), 1) == pos[...]).astype(bf16)
    x32 = dot(hot, fetched[...])
    x = x32.astype(bf16)
    x_out[...] = x
    row_sent = lax.broadcasted_iota(jnp.int32, (span, span), 0) // seq
    col_sent = lax.broadcasted_iota(jnp.int32, (span, span), 1) // seq
    same = row_sent == col_sent
    res = x32 + vec[0:1, :]
    for r, a in enumerate((a0, a1, a2, a3)):
        bias = a[width : width + 16, :].astype(f32)
        bias_out[r : r + 1, :] = bias[1:2, :]
        mixed = dot(x, a[0:width, 0 : 3 * hc])
        q = (mixed[:, 0:hc] + bias[0:1, 0:hc]).astype(bf16)
        k = mixed[:, hc : 2 * hc].astype(bf16)
        v = (mixed[:, 2 * hc : 3 * hc] + bias[0:1, hc : 2 * hc]).astype(bf16)
        qkv_out[r, 0] = q
        qkv_out[r, 1] = k
        qkv_out[r, 2] = v
        for p in range(spans):
            rows = slice(p * span, (p + 1) * span)
            ctx = jnp.zeros((span, hc), f32)
            for h in range(heads):
                mask = head_mask(span, hc, h)
                s = dot_nt(q[rows] * mask, k[rows]) * HEAD_DIM ** (-0.5)
                s = jnp.where(same, s, masked_out)
                e = jnp.exp(s - jnp.max(s, axis=1, keepdims=True))
                prob = e / jnp.sum(e, axis=1, keepdims=True)
                prob_out[(r * spans + p) * heads + h] = prob
                ctx = ctx + dot(prob.astype(bf16), v[rows] * mask)
            ctx_out[r, rows, :] = ctx.astype(bf16)
        res = res + dot_nt(ctx_out[r], a[0:width, 3 * hc : 3 * hc + hc])
    centre = res - mean_rows(res)
    inverse = lax.rsqrt(mean_rows(centre * centre) + norm_eps)
    norm_out[...] = centre * inverse
    inv_out[...] = inverse


def ffn_kernel(
    seq, norm1, vec, f0, f1, f2, f3, biases,
    h_out, act_out, slope_out, hid_out, norm_out, inv_out, cls_out, pool_out, first, h, up, acc,
):
    tok, width = norm1.shape
    cols = act_out.shape[2]
    step = 32
    g1, s1 = vec[1:2, :], vec[2:3, :]

    def chunk(i):
        return pl.ds(pl.multiple_of(i * step, step), step)

    @pl.loop(0, tok // step)
    def _(i):
        v = norm1[chunk(i), :] * g1 + s1
        first[chunk(i), :] = v
        h[chunk(i), :] = v.astype(bf16)

    h_out[...] = h[...]
    for r, f in enumerate((f0, f1, f2, f3)):
        bias = biases[r : r + 1, :]
        up[...] = dot(h[...], f[0:width, :])

        @pl.loop(0, tok // step)
        def _(i, r=r, bias=bias):
            u = up[chunk(i), :] + bias
            cdf = 0.5 * (1.0 + lax.erf(u * root_half))
            act_out[r, chunk(i), :] = (u * cdf).astype(bf16)
            slope_out[r, chunk(i), :] = cdf + u * jnp.exp(-0.5 * u * u) * inv_root_tau

        part = dot(act_out[r], f[width:, :])
        if r == 0:
            acc[...] = part
        else:
            acc[...] += part
    bo, g2, s2 = vec[3:4, :], vec[4:5, :], vec[5:6, :]

    @pl.loop(0, tok // step)
    def _(i):
        res = first[chunk(i), :] + acc[chunk(i), :] + bo
        centre = res - mean_rows(res)
        inverse = lax.rsqrt(mean_rows(centre * centre) + norm_eps)
        normed = centre * inverse
        norm_out[chunk(i), :] = normed
        inv_out[chunk(i), :] = inverse
        hid_out[chunk(i), :] = normed * g2 + s2

    sent = pool_out.shape[0]
    for s in range(sent):
        cls_out[s : s + 1, :] = hid_out[s * seq : s * seq + 1, :]
    c = cls_out[...]
    radius = lax.rsqrt(jnp.sum(c * c, axis=-1, keepdims=True) + norm_eps)
    pool_out[...] = (c * radius).astype(bf16)


def back_ffn_kernel(
    seq, pooled, pair, pair_own, cls, grad_out, norm2, inv2, vec, h, act, slope, f0, f1, f2, f3,
    loss_out, dfirst_out, keep_out, send_out, sum_out, dh, dffn, dup, dact,
):
    tok, width = grad_out.shape
    cols = act.shape[2]
    pairs = pair.shape[0]
    sents = pooled.shape[0]
    sent = cls.shape[0]
    step = 32
    every = pooled[...]
    lane = lax.broadcasted_iota(jnp.int32, (pairs, sents), 1)
    source = dot((lane == pair[:, 0:1]).astype(bf16), every)
    target = dot((lane == pair[:, 1:2]).astype(bf16), every)
    at_row = lax.broadcasted_iota(jnp.int32, (pairs, pairs), 0)
    at_col = lax.broadcasted_iota(jnp.int32, (pairs, pairs), 1)
    eye = (at_row == at_col).astype(f32)
    logits = score_scale * (dot_nt(source.astype(bf16), target.astype(bf16)) - margin * eye)
    row_peak = jnp.max(logits, axis=1, keepdims=True)
    row_exp = jnp.exp(logits - row_peak)
    row_sum = jnp.sum(row_exp, axis=1, keepdims=True)
    col_peak = jnp.max(logits, axis=0, keepdims=True)
    col_exp = jnp.exp(logits - col_peak)
    col_sum = jnp.sum(col_exp, axis=0, keepdims=True)
    total = (
        0.5 * jnp.sum(row_peak + jnp.log(row_sum), axis=0, keepdims=True)
        + 0.5 * jnp.sum(col_peak + jnp.log(col_sum), axis=1, keepdims=True)
        - jnp.sum(jnp.sum(logits * eye, axis=1, keepdims=True), axis=0, keepdims=True)
    )
    loss_out[...] = total / pairs
    d_logits = 0.5 * (row_exp / row_sum + col_exp / col_sum) - eye
    own = lax.broadcasted_iota(jnp.int32, (8, pairs), 0)
    own_source = (own == pair_own[0:1, :]).astype(f32)
    own_target = (own == pair_own[1:2, :]).astype(f32)
    from_source = jnp.dot(own_source, d_logits, precision=highest_value, preferred_element_type=f32)
    from_target = lax.dot_general(
        own_target, d_logits, (((1,), (1,)), ((), ())), precision=highest_value,
        preferred_element_type=f32,
    )
    d_pooled = score_scale * (
        jnp.dot(from_source, target, precision=highest_value, preferred_element_type=f32)
        + jnp.dot(from_target, source, precision=highest_value, preferred_element_type=f32)
    )[0:sent]
    c = cls[...]
    radius = lax.rsqrt(jnp.sum(c * c, axis=-1, keepdims=True) + norm_eps)
    d_cls = radius * d_pooled - c * radius * radius * radius * jnp.sum(
        c * d_pooled, axis=-1, keepdims=True
    )
    dh[...] = grad_out[...]
    for s in range(sent):
        dh[s * seq : s * seq + 1, :] += d_cls[s : s + 1, :]
    g2 = vec[4:5, :]

    def chunk(i):
        return pl.ds(pl.multiple_of(i * step, step), step)

    zero = jnp.zeros((1, width), f32)

    def norm_back(i, sums):
        grad = dh[chunk(i), :]
        normed = norm2[chunk(i), :]
        e = grad * g2
        d_res = (e - mean_rows(e) - normed * mean_rows(e * normed)) * inv2[chunk(i), :]
        dfirst_out[chunk(i), :] = d_res
        dffn[chunk(i), :] = d_res.astype(bf16)
        return (
            sums[0] + jnp.sum(d_res, axis=0, keepdims=True),
            sums[1] + jnp.sum(grad * normed, axis=0, keepdims=True),
            sums[2] + jnp.sum(grad, axis=0, keepdims=True),
        )

    sums = lax.fori_loop(0, tok // step, norm_back, (zero, zero, zero))
    for i in range(3):
        sum_out[i : i + 1, :] = sums[i]
    sum_out[7:8, :] = zero
    d_ffn_t = dffn[...].T
    h_t = h[...].T
    for r, f in enumerate((f0, f1, f2, f3)):
        dact[...] = dot_nt(dffn[...], f[width:, :])

        def through(i, total, r=r):
            d_up = (dact[chunk(i), :] * slope[r, chunk(i), :]).astype(bf16)
            dup[chunk(i), :] = d_up
            return total + jnp.sum(d_up.astype(f32), axis=0, keepdims=True)

        sum_out[3 + r : 4 + r, :] = lax.fori_loop(
            0, tok // step, through, jnp.zeros((1, cols), f32)
        )
        dfirst_out[...] += dot_nt(dup[...], f[0:width, :])
        out = send_out if r % 2 else keep_out
        out[r // 2, 0] = dot(h_t, dup[...]).astype(bf16)
        out[r // 2, 1] = dot(d_ffn_t, act[r]).astype(bf16)


def back_attend_kernel(
    seq, dfirst, norm1, inv1, vec, x, qkv, prob, ctx, pos, a0, a1, a2, a3,
    keep_out, send_out, slot_out, sum_out, head_out, datt, dres,
):
    tok, width = dfirst.shape
    hc = ctx.shape[2]
    heads = hc // HEAD_DIM
    span = 2 * seq
    spans = tok // span
    step = 32
    g1 = vec[1:2, :]

    def chunk(i):
        return pl.ds(pl.multiple_of(i * step, step), step)

    zero = jnp.zeros((1, width), f32)

    def norm_back(i, sums):
        grad = dfirst[chunk(i), :]
        normed = norm1[chunk(i), :]
        e = grad * g1
        d_res = (e - mean_rows(e) - normed * mean_rows(e * normed)) * inv1[chunk(i), :]
        dres[chunk(i), :] = d_res
        datt[chunk(i), :] = d_res.astype(bf16)
        return (
            sums[0] + jnp.sum(d_res, axis=0, keepdims=True),
            sums[1] + jnp.sum(grad * normed, axis=0, keepdims=True),
            sums[2] + jnp.sum(grad, axis=0, keepdims=True),
        )

    sums = lax.fori_loop(0, tok // step, norm_back, (zero, zero, zero))
    for i in range(3):
        sum_out[i : i + 1, :] = sums[i]
    sum_out[3:8, :] = jnp.zeros((5, width), f32)
    d_att_t = datt[...].T
    x_t = x[...].T
    for r, a in enumerate((a0, a1, a2, a3)):
        d_ctx = dot(datt[...], a[0:width, 3 * hc : 4 * hc]).astype(bf16)
        parts = []
        for p in range(spans):
            rows = slice(p * span, (p + 1) * span)
            q, k, v = qkv[r, 0, rows, :], qkv[r, 1, rows, :], qkv[r, 2, rows, :]
            dq = jnp.zeros((span, hc), f32)
            dk, dv = dq, dq
            for h in range(heads):
                mask = head_mask(span, hc, h)
                pr = prob[(r * spans + p) * heads + h]
                dc = d_ctx[rows] * mask
                dv = dv + dot_tn(pr.astype(bf16), dc)
                dp = dot_nt(dc, v)
                ds = (pr * (dp - jnp.sum(pr * dp, axis=1, keepdims=True))).astype(bf16)
                dq = dq + dot(ds, k * mask)
                dk = dk + dot_tn(ds, q * mask)
            scale = HEAD_DIM ** (-0.5)
            parts.append(((dq * scale).astype(bf16), (dk * scale).astype(bf16), dv.astype(bf16)))
        dq, dk, dv = (jnp.concatenate([part[i] for part in parts], axis=0) for i in range(3))
        head_out[r : r + 1, :] = jnp.sum(dq.astype(f32), axis=0, keepdims=True)
        head_out[4 + r : 5 + r, :] = jnp.sum(dv.astype(f32), axis=0, keepdims=True)
        d_mixed = jnp.concatenate([dq, dk, dv], axis=1)
        dres[...] += dot_nt(d_mixed, a[0:width, 0 : 3 * hc])
        out = send_out if r % 2 else keep_out
        out[r // 2] = jnp.concatenate(
            [dot(x_t, d_mixed), dot(d_att_t, ctx[r])], axis=1
        ).astype(bf16)
    slots = slot_out.shape[0]
    hot = (lax.broadcasted_iota(jnp.int32, (slots, tok), 0) == pos[...]).astype(bf16)
    slot_out[...] = dot(hot, dres[...].astype(bf16)).astype(bf16)


def call(kernel, outs, *args, scratch=()):
    whole = pl.BlockSpec(memory_space=pltpu.VMEM)
    return pl.pallas_call(
        kernel,
        out_shape=[jax.ShapeDtypeStruct(*o) for o in outs],
        in_specs=[whole] * len(args),
        out_specs=[whole] * len(outs),
        scratch_shapes=[pltpu.VMEM(*s) for s in scratch],
        compiler_params=pltpu.CompilerParams(vmem_limit_bytes=VMEM_LIMIT),
    )(*args)


def swap(v, axis, bit):
    size = lax.axis_size(axis)
    return lax.ppermute(v, axis, [(i, i ^ bit) for i in range(size)])


def add_low(a, b):
    return (a.astype(f32) + b.astype(f32)).astype(bf16)


def sum_over_dp(v):
    n_dp = lax.axis_size("dp")
    index = lax.axis_index("dp")
    rows = v.shape[0] // n_dp
    cur = v.reshape((n_dp, rows) + v.shape[1:])
    bit = 1
    while bit < n_dp:
        cur = cur.reshape((cur.shape[0] // 2, 2) + cur.shape[1:])
        mine = (index // bit) % 2
        keep = lax.dynamic_index_in_dim(cur, mine, 1, keepdims=False)
        send = lax.dynamic_index_in_dim(cur, 1 - mine, 1, keepdims=False)
        cur = add_low(keep, swap(send, "dp", bit))
        bit *= 2
    return cur[0]


def on_device(
    token_ids,
    pair_index,
    table,
    query_key_value_weight,
    b_q,
    b_v,
    attention_output_weight,
    b_o,
    ln1_gain,
    ln1_bias,
    feed_input_weight,
    feed_input_bias,
    feed_output_weight,
    b_out,
    ln2_gain,
    ln2_bias,
    grad_out,
):
    sent, seq = token_ids.shape
    tok = sent * seq
    rows_shard, width = table.shape
    shards = lax.axis_size(("dp", "mp"))
    n_mp = lax.axis_size("mp")
    capacity = 2 * tok // shards
    slots = shards * capacity
    hc = query_key_value_weight.shape[2]
    cols = feed_input_weight.shape[1]
    heads = hc // HEAD_DIM
    spans = tok // (2 * seq)

    bias_rows = jnp.zeros((16, width), bf16)
    bias_rows = bias_rows.at[0, 0:hc].set(b_q).at[0, hc : 2 * hc].set(b_v)
    bias_rows = bias_rows.at[1, 0:cols].set(feed_input_bias)
    own_a = jnp.concatenate(
        [
            jnp.concatenate(
                [query_key_value_weight.reshape(width, 3 * hc), attention_output_weight.T], axis=1
            ),
            bias_rows,
        ],
        axis=0,
    )
    own_f = jnp.concatenate([feed_input_weight, feed_output_weight], axis=0)
    a_x = swap(own_a, "mp", 2)
    f_x = swap(own_f, "mp", 2)
    a_all = (own_a, swap(own_a, "mp", 1), a_x, swap(a_x, "mp", 1))
    f_all = (own_f, swap(own_f, "mp", 1), f_x, swap(f_x, "mp", 1))

    flat_ids = token_ids.reshape(tok)
    owners = flat_ids // rows_shard
    within = flat_ids - owners * rows_shard
    order = jnp.arange(tok, dtype=jnp.int32)
    earlier = (owners[:, None] == owners[None, :]) & (order[None, :] < order[:, None])
    pos = owners * capacity + jnp.sum(earlier.astype(jnp.int32), axis=1)
    hit = jnp.arange(slots, dtype=jnp.int32)[:, None] == pos[None, :]
    requests = jnp.sum(jnp.where(hit, within[None, :] + 1, 0), axis=1) - 1
    requests = requests.reshape(shards, capacity)
    asked = lax.all_to_all(requests, ("dp", "mp"), split_axis=0, concat_axis=0, tiled=True)
    picked = jnp.take(table, jnp.maximum(asked, 0), axis=0)
    fetched = lax.all_to_all(picked, ("dp", "mp"), split_axis=0, concat_axis=0, tiled=True)

    vec = jnp.stack([b_o, ln1_gain, ln1_bias, b_out, ln2_gain, ln2_bias, b_o, b_o]).astype(f32)
    x, qkv, prob, ctx, norm1, inv1, biases = call(
        functools.partial(front_kernel, seq),
        [
            ((tok, width), bf16),
            ((n_mp, 3, tok, hc), bf16),
            ((n_mp * spans * heads, 2 * seq, 2 * seq), f32),
            ((n_mp, tok, hc), bf16),
            ((tok, width), f32),
            ((tok, 1), f32),
            ((n_mp, width), f32),
        ],
        fetched.reshape(slots, width),
        pos[:, None],
        *a_all,
        vec,
    )
    h, act, slope, hidden, norm2, inv2, cls, pooled = call(
        functools.partial(ffn_kernel, seq),
        [
            ((tok, width), bf16),
            ((n_mp, tok, cols), bf16),
            ((n_mp, tok, cols), f32),
            ((tok, width), f32),
            ((tok, width), f32),
            ((tok, 1), f32),
            ((sent, width), f32),
            ((sent, width), bf16),
        ],
        norm1,
        vec,
        *f_all,
        biases,
        scratch=[
            ((tok, width), f32),
            ((tok, width), bf16),
            ((tok, cols), f32),
            ((tok, width), f32),
        ],
    )
    everyone = jnp.broadcast_to(pooled[None], (shards, sent, width))
    all_pooled = lax.all_to_all(
        everyone, ("dp", "mp"), split_axis=0, concat_axis=0, tiled=True
    ).reshape(shards * sent, width)
    own_start = lax.axis_index(("dp", "mp")) * sent
    loss, d_first, keep_f, send_f, sums2 = call(
        functools.partial(back_ffn_kernel, seq),
        [
            ((1, 1), f32),
            ((tok, width), f32),
            ((2, 2, width, cols), bf16),
            ((2, 2, width, cols), bf16),
            ((8, width), f32),
        ],
        all_pooled,
        pair_index,
        pair_index.T - own_start,
        cls,
        grad_out.reshape(tok, width),
        norm2,
        inv2,
        vec,
        h,
        act,
        slope,
        *f_all,
        scratch=[
            ((tok, width), f32),
            ((tok, width), bf16),
            ((tok, cols), bf16),
            ((tok, cols), f32),
        ],
    )
    keep_a, send_a, outgoing_rows, sums1, head_sums = call(
        functools.partial(back_attend_kernel, seq),
        [
            ((2, width, 4 * hc), bf16),
            ((2, width, 4 * hc), bf16),
            ((slots, width), bf16),
            ((8, width), f32),
            ((8, hc), f32),
        ],
        d_first,
        norm1,
        inv1,
        vec,
        x,
        qkv,
        prob,
        ctx,
        pos[None, :],
        *a_all,
        scratch=[((tok, width), bf16), ((tok, width), f32)],
    )

    half_f = add_low(keep_f, swap(send_f, "mp", 1))
    half_a = add_low(keep_a, swap(send_a, "mp", 1))
    full_in = add_low(half_f[0, 0], swap(half_f[1, 0], "mp", 2))
    full_out = add_low(half_f[0, 1], swap(half_f[1, 1], "mp", 2))
    full_a = add_low(half_a[0], swap(half_a[1], "mp", 2))
    in_part = sum_over_dp(full_in).astype(f32)
    out_part = sum_over_dp(full_out).astype(f32).T
    part_a = sum_over_dp(full_a).astype(f32)
    qkv_part = part_a[:, : 3 * hc].reshape(-1, 3, hc)
    o_part = part_a[:, 3 * hc :].T

    share_cols = width // shards
    ffn_share = cols * n_mp // shards
    turn = jnp.arange(n_mp, dtype=jnp.int32) ^ lax.axis_index("mp")
    shared = jnp.concatenate(
        [
            sums1[0:3],
            sums2[0:3],
            head_sums[0:4][turn].reshape(1, width),
            head_sums[4:8][turn].reshape(1, width),
        ],
        axis=0,
    )
    outgoing = jnp.concatenate(
        [
            shared.reshape(8, shards, share_cols).transpose(1, 0, 2).reshape(shards, -1),
            sums2[3:7][turn].reshape(shards, ffn_share),
        ],
        axis=1,
    )
    arrived = lax.all_to_all(
        outgoing_rows.reshape(shards, capacity, width),
        ("dp", "mp"), split_axis=0, concat_axis=0, tiled=True,
    ).astype(f32)
    collected = lax.all_to_all(
        outgoing.astype(bf16), ("dp", "mp"), split_axis=0, concat_axis=0, tiled=True
    ).astype(f32)
    live_mask = (asked >= 0).astype(f32)[:, :, None]
    table_grad = (
        jnp.zeros((rows_shard, width), f32)
        .at[jnp.maximum(asked, 0)]
        .add(arrived * live_mask)
    )
    totals = jnp.sum(collected, axis=0)
    shared_sum = totals[: 8 * share_cols].reshape(8, share_cols)
    ffn_sum = totals[8 * share_cols :]
    return (
        hidden.reshape(sent, seq, width),
        loss[0, 0],
        table_grad,
        qkv_part,
        shared_sum[6],
        shared_sum[7],
        o_part,
        shared_sum[0],
        shared_sum[1],
        shared_sum[2],
        in_part,
        ffn_sum,
        out_part,
        shared_sum[3],
        shared_sum[4],
        shared_sum[5],
    )


def solution(mesh):
    in_specs = (
        P(("dp", "mp"), None),
        P(),
        P(("dp", "mp"), None),
        P(None, None, "mp"),
        P("mp"),
        P("mp"),
        P("mp", None),
        P(),
        P(),
        P(),
        P(None, "mp"),
        P("mp"),
        P("mp", None),
        P(),
        P(),
        P(),
        P(("dp", "mp"), None, None),
    )
    out_specs = (
        P(("dp", "mp"), None, None),
        P(),
        P(("dp", "mp"), None),
        P("dp", None, "mp"),
        P(("dp", "mp")),
        P(("dp", "mp")),
        P("mp", "dp"),
        P(("dp", "mp")),
        P(("dp", "mp")),
        P(("dp", "mp")),
        P("dp", "mp"),
        P(("dp", "mp")),
        P("mp", "dp"),
        P(("dp", "mp")),
        P(("dp", "mp")),
        P(("dp", "mp")),
    )
    return jax.shard_map(
        on_device, mesh=mesh, in_specs=in_specs, out_specs=out_specs, check_vma=False
    )
```
